32 devices in a mesh: dp: 4 (over y, core), seq: 8 (over z, x).
Axes of the slice: x: 2, y: 2, z: 4, core: 2. Of those that a mesh axis runs over, the one named last changes fastest.
Arguments:
- source_embed: bfloat16 [2, 4, 1024, 1024], P(None, 'dp', 'seq'), may hold values from -6 to 6
- target_embed: bfloat16 [2, 4, 1024, 1024], P(None, 'dp', 'seq'), may hold values from -6 to 6
- source_docs: int32 [2, 4, 1024], P(None, 'dp', 'seq'), may hold values from 0 to 2, as said below
- target_docs: int32 [2, 4, 1024], P(None, 'dp', 'seq'), may hold values from 0 to 2, as said below
- label_index: int32 [2, 4, 48], P(None, 'dp', 'seq'), may hold values from 0 to 1023, as said below
- label_token: int32 [2, 4, 48], P(None, 'dp', 'seq'), may hold values from 0 to 32767
- attend_in: bfloat16 [3, 3, 1024, 1024], P(None, None, ('dp', 'seq')), may hold values from -0.1875 to 0.1875
- attend_out: bfloat16 [3, 1024, 1024], P(None, ('dp', 'seq')), may hold values from -0.75 to 0.75
- feed_up: bfloat16 [2, 1024, 4096], P(None, ('dp', 'seq')), may hold values from -0.1875 to 0.1875
- feed_down: bfloat16 [2, 4096, 1024], P(None, ('dp', 'seq')), may hold values from -0.09375 to 0.09375
- norm_gain: bfloat16 [9, 1024], P(None, ('dp', 'seq')), may hold values from 0.25 to 1.75
- norm_bias: bfloat16 [9, 1024], P(None, ('dp', 'seq')), may hold values from -2.5 to 2.5
- vocab_table: bfloat16 [32768, 1024], P(('dp', 'seq')), may hold values from -0.1875 to 0.1875
Outputs:
- mean_loss: float32 [], replicated
- source_grad: float32 [2, 4, 1024, 1024], P(None, 'dp', 'seq')
- target_grad: float32 [2, 4, 1024, 1024], P(None, 'dp', 'seq')
- attend_in_grad: float32 [3, 3, 1024, 1024], P(None, None, ('dp', 'seq'))
- attend_out_grad: float32 [3, 1024, 1024], P(None, ('dp', 'seq'))
- feed_up_grad: float32 [2, 1024, 4096], P(None, ('dp', 'seq'))
- feed_down_grad: float32 [2, 4096, 1024], P(None, ('dp', 'seq'))
- norm_gain_grad: float32 [9, 1024], P(None, ('dp', 'seq'))
- norm_bias_grad: float32 [9, 1024], P(None, ('dp', 'seq'))
- vocab_table_grad: float32 [32768, 1024], P(('dp', 'seq'))
The draws below stay inside these ranges and needn't reach their ends.
Inputs may be any that keep to these rules, and one draw needn't show every extreme that they name: `source_docs`: each row holds the documents 0, 1 and 2 in this order; document 0 ends within the first 128 positions, document 2 begins within the last 128 positions. `target_docs`: each row holds the documents 0, 1 and 2 in this order; document 0 ends within the first 128 positions, document 2 begins within the last 128 positions. `label_index`: entries k * 6 to (k + 1) * 6 - 1 of a row are distinct positions from k * 128 to (k + 1) * 128 - 1; the first and the last position of every row carry a label.
All inputs are finite; a program needn't handle non-finite values.
Results may differ from the reference program's by a relative error of at most 0.015.
Values may be sent and summed in bfloat16 or wider, within the bound.
No kernel may reach another device: no remote copies, remote signals or barrier semaphores. Data moves between devices by JAX's collectives and lax.ppermute only.
A program may use at most 448 MiB of HBM per device.

```python
import math
import jax
import jax.numpy as jnp
from jax import lax

D = 1024
HEADS = 16
HEAD = 64
FF = 4096
NORMS = 9
MICRO = 2
LAB_DEV = 6
ROWS = 4
ROW_LEN = 1024
SPAN = 128
LABELS = 48
VOCAB = 32768


def documents_from(key):
    first_key, last_key = jax.random.split(key)
    first_len = jax.random.randint(first_key, (MICRO, ROWS, 1), 1, SPAN)
    last_len = jax.random.randint(last_key, (MICRO, ROWS, 1), 1, SPAN)
    places = jnp.arange(ROW_LEN, dtype=jnp.int32)[None, None, :]
    return ((places >= first_len).astype(jnp.int32) + (places >= ROW_LEN - last_len).astype(jnp.int32)).astype(jnp.int32)


def draw_source_docs(key, part):
    key = jax.random.fold_in(key, 11)
    return documents_from(key)


def draw_target_docs(key, part):
    key = jax.random.fold_in(key, 12)
    return documents_from(key)


def draw_label_index(key, part):
    key = jax.random.fold_in(key, 13)
    blocks = ROW_LEN // SPAN
    ranks = jax.random.randint(key, (MICRO, ROWS, blocks, SPAN), 0, 4096) * SPAN
    ranks = ranks + jnp.arange(SPAN, dtype=jnp.int32)
    ranks = ranks.at[:, :, 0, 0].set(4097 * SPAN)
    ranks = ranks.at[:, :, blocks - 1, SPAN - 1].set(4097 * SPAN)
    offsets = lax.top_k(ranks, LAB_DEV)[1].astype(jnp.int32)
    starts = (jnp.arange(blocks, dtype=jnp.int32) * SPAN)[None, None, :, None]
    return (offsets + starts).reshape(MICRO, ROWS, blocks * LAB_DEV).astype(jnp.int32)


def set_ends(values, own_key, low, top_value):
    longest = values.shape.index(max(values.shape))
    spots = []
    for shift in (0, 1):
        where = [jax.random.randint(jax.random.fold_in(own_key, axis), (), 0, length) for axis, length in enumerate(values.shape)]
        where[longest] = (where[longest] + shift) % values.shape[longest]
        spots.append(tuple(where))
    return values.at[spots[0]].set(low).at[spots[1]].set(top_value)


def levels(stream_key, shape, pieces, low, high):
    loudness = 1.0
    for dim, parts in pieces:
        steps = jax.random.uniform(jax.random.fold_in(jax.random.fold_in(stream_key, 6), dim), (parts,), jnp.float32, low / len(pieces), high / len(pieces))
        loudness = loudness * jnp.repeat(jnp.exp(steps), shape[dim] // parts).reshape((-1,) + (1,) * (len(shape) - 1 - dim))
    return loudness


def centred(rng, shape, scale, most, shards=(), kind=jnp.bfloat16):
    drawn = jax.random.normal(rng, shape, jnp.float32) * scale
    if len(shards) > 0:
        drawn = levels(rng, shape, shards, -0.22, 0.18) * drawn
    return jnp.clip(drawn, min=-most, max=most).astype(kind)


def setup_inputs(seed: int = 0) -> dict:
    key_of = jax.random.split(jax.random.key(seed), 14)
    return {
        "source_embed": centred(key_of[0], (MICRO, ROWS, ROW_LEN, D), 1.0, 6.0, ((1, 4), (2, 8))),
        "target_embed": centred(key_of[1], (MICRO, ROWS, ROW_LEN, D), 1.0, 6.0, ((1, 4), (2, 8))),
        "source_docs": draw_source_docs(jax.random.fold_in(key_of[13], 71), 0),
        "target_docs": draw_target_docs(jax.random.fold_in(key_of[13], 71), 0),
        "label_index": draw_label_index(jax.random.fold_in(key_of[13], 71), 0),
        "label_token": set_ends(jax.random.randint(key_of[5], (MICRO, ROWS, LABELS), 0, VOCAB), jax.random.fold_in(key_of[5], 1), 0, VOCAB - 1).astype(jnp.int32),
        "attend_in": centred(key_of[6], (3, 3, D, D), D ** -0.5, 0.1875, ((2, 32),)),
        "attend_out": centred(key_of[7], (3, D, D), (D // 16) ** -0.5, 0.75, ((1, 32),)),
        "feed_up": centred(key_of[8], (2, D, FF), D ** -0.5, 0.1875, ((1, 32),)),
        "feed_down": centred(key_of[9], (2, FF, D), FF ** -0.5, 0.09375, ((1, 32),)),
        "norm_gain": jnp.clip(1.0 + 0.15 * jax.random.normal(key_of[10], (NORMS, D), jnp.float32), 0.25, 1.75).astype(jnp.bfloat16),
        "norm_bias": centred(key_of[11], (NORMS, D), 0.3, 2.5, ((1, 32),)),
        "vocab_table": centred(key_of[12], (VOCAB, D), D ** -0.5, 0.1875, ((0, 32),)),
    }


EPSILON = 1e-05
MASK_VALUE = -1000000000.0
HIGHEST = lax.Precision.HIGHEST

@jax.custom_vjp
def low(v):
    return lax.optimization_barrier(v.astype(jnp.bfloat16)).astype(jnp.float32)

@jax.custom_vjp
def low_back(v):
    return v

def low_keep(v):
    return (low(v), None)

def low_pass(kept, grad):
    return (grad,)

def back_keep(v):
    return (v, None)

def back_low(kept, grad):
    return (low(grad),)
low.defvjp(low_keep, low_pass)
low_back.defvjp(back_keep, back_low)

def layer_norm(values, gain_row, bias_row):
    center = lax.optimization_barrier(jnp.mean(values, axis=-1, keepdims=True))
    shifted = values - center
    spread = lax.optimization_barrier(jnp.mean(shifted * shifted, axis=-1, keepdims=True))
    return shifted * lax.rsqrt(spread + EPSILON) * gain_row + bias_row

def project(left, right):
    return jnp.dot(left, right, precision=HIGHEST)

def attend(query_in, key_in, weight_in, weight_out, key_mask):
    query_len = query_in.shape[0]
    key_len = key_in.shape[0]
    queries = low_back(low(project(query_in, weight_in[0]))).reshape(query_len, HEADS, HEAD)
    all_keys = low_back(low(project(key_in, weight_in[1]))).reshape(key_len, HEADS, HEAD)
    values = low_back(low(project(key_in, weight_in[2]))).reshape(key_len, HEADS, HEAD)
    scores = jnp.einsum('qhd,khd->hqk', queries, all_keys, precision=HIGHEST) * (1.0 / math.sqrt(HEAD))
    scores = jnp.where(key_mask[None], low_back(scores), MASK_VALUE)
    attention = low(jax.nn.softmax(scores, axis=-1))
    mixed_heads = jnp.einsum('hqk,khd->qhd', attention, values, precision=HIGHEST).reshape(query_len, HEADS * HEAD)
    mixed_heads = low_back(low(mixed_heads))
    return low_back(project(mixed_heads, weight_out))

def feed_forward(residual, gain_row, bias_row, weight_up, weight_down):
    normed = low(layer_norm(residual, gain_row, bias_row))
    up_proj = low_back(project(normed, weight_up))
    hidden = low(jax.nn.gelu(up_proj, approximate=False))
    return low_back(project(hidden, weight_down))

def row_loss(params, source_row, target_row, source_row_docs, target_row_docs, label_row_index, label_row_token):
    weight_in, weight_out, weight_up, weight_down, gains, biases, table = params
    places = jnp.arange(ROW_LEN)
    enc_start = layer_norm(source_row, gains[0], biases[0])
    enc_normed = low(layer_norm(enc_start, gains[1], biases[1]))
    enc_mask = source_row_docs[:, None] == source_row_docs[None, :]
    enc_middle = enc_start + attend(enc_normed, enc_normed, weight_in[0], weight_out[0], enc_mask)
    enc_end = enc_middle + feed_forward(enc_middle, gains[2], biases[2], weight_up[0], weight_down[0])
    encoded = low(layer_norm(enc_end, gains[3], biases[3]))
    dec_start = layer_norm(target_row, gains[4], biases[4])
    dec_normed = low(layer_norm(dec_start, gains[5], biases[5]))
    self_mask = (target_row_docs[:, None] == target_row_docs[None, :]) & (places[None, :] <= places[:, None])
    dec_self = dec_start + attend(dec_normed, dec_normed, weight_in[1], weight_out[1], self_mask)
    cross_normed = low(layer_norm(dec_self, gains[6], biases[6]))
    cross_mask = target_row_docs[:, None] == source_row_docs[None, :]
    dec_cross = dec_self + attend(cross_normed, encoded, weight_in[2], weight_out[2], cross_mask)
    dec_end = dec_cross + feed_forward(dec_cross, gains[7], biases[7], weight_up[1], weight_down[1])
    final = layer_norm(dec_end, gains[8], biases[8])
    picked = low(jnp.take(final, label_row_index, axis=0))
    logits = low_back(jnp.dot(picked, table.T, precision=HIGHEST))
    log_total = jax.nn.logsumexp(logits, axis=-1)
    target_logit = jnp.take_along_axis(logits, label_row_token[:, None], axis=1)[:, 0]
    return jnp.sum(log_total - target_logit)

def reference(source_embed, target_embed, source_docs, target_docs, label_index, label_token, attend_in, attend_out, feed_up, feed_down, norm_gain, norm_bias, vocab_table):
    row_count = MICRO * ROWS
    source = source_embed.astype(jnp.float32).reshape(row_count, ROW_LEN, D)
    target = target_embed.astype(jnp.float32).reshape(row_count, ROW_LEN, D)
    integers = (source_docs.reshape(row_count, ROW_LEN), target_docs.reshape(row_count, ROW_LEN), label_index.reshape(row_count, LABELS), label_token.reshape(row_count, LABELS))
    params = (attend_in.astype(jnp.float32), attend_out.astype(jnp.float32), feed_up.astype(jnp.float32), feed_down.astype(jnp.float32), norm_gain.astype(jnp.float32), norm_bias.astype(jnp.float32), vocab_table.astype(jnp.float32))

    def total_loss(source_all, target_all, weights):

        def accumulate(running, row_item):
            return (running + jax.checkpoint(row_loss)(weights, *row_item), None)
        summed_rows, unused = lax.scan(accumulate, jnp.zeros((), jnp.float32), (source_all, target_all) + integers)
        return summed_rows
    summed, pull = jax.vjp(total_loss, source, target, params)
    grad_source, grad_target, grad_params = pull(jnp.ones((), jnp.float32))
    mean_loss = summed / (row_count * LABELS)
    return (mean_loss, grad_source.reshape(MICRO, ROWS, ROW_LEN, D), grad_target.reshape(MICRO, ROWS, ROW_LEN, D), grad_params[0], grad_params[1], grad_params[2], grad_params[3], grad_params[4], grad_params[5], grad_params[6])
```

```python
import functools
import math

import jax
import jax.numpy as jnp
from jax import lax
from jax.experimental import pallas as pl
from jax.experimental.pallas import tpu as pltpu
from jax.sharding import PartitionSpec as P

HEADS = 16
HEAD = 64

EPSILON = 1e-05
MASK_VALUE = -1000000000.0
AXES = ("r", "c", "a", "i", "b")
MEMBERS = ("c", "i")
BF16 = jnp.bfloat16
F32 = jnp.float32


def product(left, right):
    return jnp.dot(left, right, preferred_element_type=F32)


def by_transpose(left, right):
    return lax.dot_general(left, right, (((1,), (1,)), ((), ())), preferred_element_type=F32)


def rows_inner(left, right):
    return lax.dot_general(left, right, (((0,), (0,)), ((), ())), preferred_element_type=F32)


def tie(value, *others):
    return lax.optimization_barrier((value,) + others)[0]


class Grid:
    def __init__(self, dp, seq):
        self.R, self.C, self.A, self.B = dp // 2, 2, 2, 2
        self.I = seq // 4
        self.n = dp * seq
        self.G = self.C * self.I
        self.K = self.R * self.A * self.B

    def flat(self, r, c, a, i, b):
        return (((r * 2 + c) * 2 + a) * self.I + i) * 2 + b

    def here(self):
        me = lax.axis_index(AXES)
        self.me = me
        self.b = me % 2
        self.i = (me // 2) % self.I
        self.a = (me // (2 * self.I)) % 2
        self.c = (me // (4 * self.I)) % 2
        self.r = me // (8 * self.I)

    def send(self, array, move):
        pairs = []
        for r in range(self.R):
            for c in range(2):
                for a in range(2):
                    for i in range(self.I):
                        for b in range(2):
                            pairs.append(
                                (self.flat(r, c, a, i, b), self.flat(*move(r, c, a, i, b)))
                            )
        return lax.ppermute(array, AXES, pairs)

    def everyone(self, row):
        return lax.all_to_all(jnp.broadcast_to(row[None], (self.n,) + row.shape), AXES, 0, 0)

    def swap_cores(self, array):
        return self.send(array, lambda r, c, a, i, b: (r, 1 - c, a, i, b))

    def far_chips(self, own):
        return [
            self.send(own, lambda r, c, a, i, b: (r, c, a, (i - di) % self.I, b))
            for di in range(1, self.I)
        ]

    def both_cores(self, array):
        return jnp.concatenate([array, self.swap_cores(array)])

    def join_cores(self, part):
        half = part.shape[0] // 2
        return part[:half] + self.swap_cores(part[half:].astype(BF16)).astype(F32)

    def return_chip(self, joint, di):
        return self.send(
            joint.astype(BF16), lambda r, c, a, i, b: (r, c, a, (i + di) % self.I, b)
        )

    def exchange(self, blocks):
        return lax.all_to_all(blocks, MEMBERS, 0, 0)

    def steps(self, order):
        found = []
        for name in order:
            if name == "a":
                found.append((1, 0, self.a, lambda r, c, a, i, b: (r, c, 1 - a, i, b)))
            elif name == "b":
                found.append((2, 0, self.b, lambda r, c, a, i, b: (r, c, a, i, 1 - b)))
            else:
                for bit in range(int(math.log2(self.R))):
                    found.append(
                        (
                            0,
                            bit,
                            (self.r >> bit) & 1,
                            lambda r, c, a, i, b, bit=bit: (r ^ (1 << bit), c, a, i, b),
                        )
                    )
        return found


class Gathering:
    def __init__(self, grid, piece, order):
        self.grid, self.gathered, self.got = grid, piece[None], None
        self.moves = grid.steps(order)
        self.places = [(0, 0, 0)]

    def land(self, after):
        if self.got is not None:
            self.gathered = jnp.concatenate([self.gathered, tie(self.got, *after)])
            self.got = None

    def step(self, *after):
        self.land(after)
        axis, bit, unused, move = self.moves.pop(0)
        self.got = self.grid.send(tie(self.gathered, *after), move)
        moved = tuple((1 << bit) if axis == j else 0 for j in range(3))
        self.places = self.places + [
            tuple(p ^ q for p, q in zip(place, moved)) for place in self.places
        ]

    def finish(self, *after):
        while self.moves:
            self.step(*after)
        self.land(after)
        grid, found_at = self.grid, []
        for r in range(grid.R):
            for a in range(2):
                for b in range(2):
                    index = 0
                    for k, (pr, pa, pb) in enumerate(self.places):
                        found = ((grid.r ^ pr) == r) & ((grid.a ^ pa) == a) & ((grid.b ^ pb) == b)
                        index = index + jnp.where(found, k, 0)
                    found_at.append(index)
        return self.gathered, jnp.stack(found_at).astype(jnp.int32)


class Scattering:
    def __init__(self, grid, parts, order, axes):
        self.grid, self.parts, self.got = grid, parts, None
        self.moves = [
            (axes[axis], up, move) for axis, bit, up, move in reversed(grid.steps(order))
        ]

    def land(self, after):
        if self.got is not None:
            self.parts = self.keep.astype(F32) + tie(self.got, *after).astype(F32)
            self.got = None

    def step(self, *after):
        self.land(after)
        axis, up, move = self.moves.pop(0)
        half = self.parts.shape[axis] // 2
        self.keep = lax.dynamic_slice_in_dim(self.parts, up * half, half, axis)
        give = lax.dynamic_slice_in_dim(self.parts, (1 - up) * half, half, axis)
        self.got = self.grid.send(give.astype(BF16), move)

    def finish(self, *after):
        while self.moves:
            self.step(*after)
        self.land(after)
        return self.parts


class Order:
    def __init__(self):
        self.last = None

    def use(self, value):
        return value if self.last is None else tie(value, self.last)

    def did(self, value):
        self.last = value
        return value


def normalized(values):
    center = jnp.mean(values, axis=-1, keepdims=True)
    shifted = values - center
    spread = jnp.mean(shifted * shifted, axis=-1, keepdims=True)
    rate = lax.rsqrt(spread + EPSILON)
    return shifted * rate, rate


def layer_norm(values, gain, bias):
    unit, rate = normalized(values)
    return unit * gain + bias


def norm_back(values, gain, gradient):
    unit, rate = normalized(values)
    scaled = gradient * gain
    mean_grad = jnp.mean(scaled, axis=-1, keepdims=True)
    mean_along = jnp.mean(scaled * unit, axis=-1, keepdims=True)
    return (
        rate * (scaled - mean_grad - unit * mean_along),
        jnp.sum(gradient * unit, axis=0),
        jnp.sum(gradient, axis=0),
    )


def gelu_gate(values):
    return 0.5 + 0.5 * lax.erf(values * math.sqrt(0.5))


def gelu_slope(values):
    density = jnp.exp(-0.5 * values * values) * (1.0 / math.sqrt(2.0 * math.pi))
    return gelu_gate(values) + values * density


LANES = 128
SCALE = 1.0 / math.sqrt(HEAD)


def in_head(values, head):
    lane = lax.broadcasted_iota(jnp.int32, values.shape, 1)
    inside = (lane >= head * HEAD) & (lane < (head + 1) * HEAD)
    return jnp.where(inside, values, jnp.zeros_like(values))


def inner(left, right, left_dim, right_dim):
    return lax.dot_general(
        left, right, (((left_dim,), (right_dim,)), ((), ())), preferred_element_type=F32
    )


def allowed(causal, key_docs, query_docs, key_places, query_places):
    mask = key_docs[...] == query_docs[...]
    if causal:
        mask = mask & (key_places[...] <= query_places[...])
    return mask


def head_rows(values, head):
    row = lax.broadcasted_iota(jnp.int32, values.shape, 0)
    inside = (row >= head * HEAD) & (row < (head + 1) * HEAD)
    return jnp.where(inside, values, jnp.zeros_like(values))


def turned(values):
    return jnp.transpose(values.astype(F32)).astype(values.dtype)


def attend_kernel(
    causal, q, k, v, key_docs, query_docs, key_places, query_places, mixed, log_total, v_turned
):
    @pl.when(pl.program_id(1) == 0)
    def turn():
        v_turned[...] = turned(v[...])

    mask = allowed(causal, key_docs, query_docs, key_places, query_places)
    queries = q[...] * jnp.asarray(SCALE, BF16)
    result = None
    for head in range(LANES // HEAD):
        scores = inner(k[...], in_head(queries, head), 1, 1)
        scores = jnp.where(mask, scores, MASK_VALUE)
        row_max = jnp.max(scores, axis=0, keepdims=True)
        exponent = jnp.exp(scores - row_max)
        row_sum = jnp.sum(exponent, axis=0, keepdims=True)
        attention = (exponent * (1.0 / row_sum)).astype(BF16)
        part = head_rows(inner(v_turned[...], attention, 1, 0), head)
        result = part if result is None else result + part
        log_total[0, head : head + 1, :] = row_max + jnp.log(row_sum)
    mixed[...] = jnp.transpose(result).astype(BF16)


def attend_back_kernel(
    causal,
    q,
    k,
    v,
    key_docs,
    query_docs,
    key_places,
    query_places,
    log_total,
    grad_mixed,
    grads,
    grad_keys,
    grad_values,
    k_turned,
):
    pair, tile = pl.program_id(0), pl.program_id(1)
    pairs, tiles = pl.num_programs(0), pl.num_programs(1)
    size = q.shape[0]

    @pl.when(tile == 0)
    def clear():
        grad_keys[...] = jnp.zeros_like(grad_keys)
        grad_values[...] = jnp.zeros_like(grad_values)
        k_turned[...] = turned(k[...])

    mask = allowed(causal, key_docs, query_docs, key_places, query_places)
    queries = q[...] * jnp.asarray(SCALE, BF16)
    grad_queries = None
    for head in range(LANES // HEAD):
        head_queries = in_head(queries, head)
        head_grad = in_head(grad_mixed[...], head)
        scores = jnp.where(mask, inner(k[...], head_queries, 1, 1), MASK_VALUE)
        attention = jnp.exp(scores - log_total[0, head : head + 1, :])
        grad_attention = inner(v[...], head_grad, 1, 1)
        row_delta = jnp.sum(attention * grad_attention, axis=0, keepdims=True)
        grad_scores = (attention * (grad_attention - row_delta)).astype(BF16)
        grad_values[...] += inner(attention.astype(BF16), head_grad, 1, 0)
        grad_keys[...] += inner(grad_scores, head_queries, 1, 0)
        part = head_rows(inner(k_turned[...], grad_scores, 1, 0), head)
        grad_queries = part if grad_queries is None else grad_queries + part

    def column(block):
        return pl.ds(pl.multiple_of(block * LANES, LANES), LANES)

    grads[pl.ds(pl.multiple_of(tile * size, size), size), column(pair)] = jnp.transpose(
        grad_queries * SCALE
    ).astype(BF16)

    @pl.when(tile == tiles - 1)
    def store():
        grads[:, column(pairs + pair)] = grad_keys[...].astype(BF16)
        grads[:, column(2 * pairs + pair)] = grad_values[...].astype(BF16)


def attend_specs(rows, tile, offsets, first):
    def keys(offset):
        return pl.BlockSpec((rows, LANES), lambda p, i: (0, offset + p))

    row = pl.BlockSpec((1, tile), lambda p, i: (0, first + i))
    column = pl.BlockSpec((rows, 1), lambda p, i: (0, 0))
    return [
        pl.BlockSpec((tile, LANES), lambda p, i: (first + i, offsets[0] + p)),
        keys(offsets[1]),
        keys(offsets[2]),
        column,
        row,
        column,
        row,
    ]


VMEM_BYTES = 48 * 1024 * 1024


def attend_call(arrays, offsets, meta, causal, part, start, count):
    rows = arrays[0].shape[0]
    pairs, tile = part // LANES, min(count, 256)
    places = [offset // LANES for offset in offsets]
    return pl.pallas_call(
        functools.partial(attend_kernel, causal),
        grid=(pairs, count // tile),
        in_specs=attend_specs(rows, tile, places, start // tile),
        out_specs=[
            pl.BlockSpec((tile, LANES), lambda p, i: (i, p)),
            pl.BlockSpec((1, LANES // HEAD, tile), lambda p, i: (p, 0, i)),
        ],
        out_shape=[
            jax.ShapeDtypeStruct((count, part), BF16),
            jax.ShapeDtypeStruct((pairs, LANES // HEAD, count), F32),
        ],
        scratch_shapes=[pltpu.VMEM((LANES, rows), BF16)],
        compiler_params=pltpu.CompilerParams(vmem_limit_bytes=VMEM_BYTES),
        cost_estimate=pl.CostEstimate(flops=0, bytes_accessed=0, transcendentals=0),
        name="attend",
    )(*arrays, *meta)


def attend_back_call(arrays, offsets, meta, causal, part, log_total, grad_mixed):
    rows = arrays[0].shape[0]
    pairs, tile = part // LANES, min(rows, 256)
    places = [offset // LANES for offset in offsets]
    return pl.pallas_call(
        functools.partial(attend_back_kernel, causal),
        grid=(pairs, rows // tile),
        in_specs=attend_specs(rows, tile, places, 0)
        + [
            pl.BlockSpec((1, LANES // HEAD, tile), lambda p, i: (p, 0, i)),
            pl.BlockSpec((tile, LANES), lambda p, i: (i, p)),
        ],
        out_specs=pl.BlockSpec((rows, 3 * part), lambda p, i: (0, 0)),
        out_shape=jax.ShapeDtypeStruct((rows, 3 * part), BF16),
        scratch_shapes=[
            pltpu.VMEM((rows, LANES), F32),
            pltpu.VMEM((rows, LANES), F32),
            pltpu.VMEM((LANES, rows), BF16),
        ],
        compiler_params=pltpu.CompilerParams(vmem_limit_bytes=VMEM_BYTES),
        cost_estimate=pl.CostEstimate(flops=0, bytes_accessed=0, transcendentals=0),
        name="attend_back",
    )(*arrays, *meta, log_total, grad_mixed)


def layout_call(kernel, outs, name, tables, arrays):
    whole = pl.BlockSpec(memory_space=pltpu.VMEM)
    return pl.pallas_call(
        kernel,
        grid_spec=pltpu.PrefetchScalarGridSpec(
            num_scalar_prefetch=len(tables),
            grid=(),
            in_specs=[whole] * len(arrays),
            out_specs=[whole] * len(outs),
        ),
        out_shape=outs,
        compiler_params=pltpu.CompilerParams(vmem_limit_bytes=VMEM_BYTES),
        cost_estimate=pl.CostEstimate(flops=0, bytes_accessed=0, transcendentals=0),
        name=name,
    )(*tables, *arrays)


def place(gathered, rows_at, outs, moves):
    def kernel(rows_ref, source, *targets):
        columns = source.shape[2]
        for out, row, column, k, first, count in moves:
            targets[out][row : row + count, column : column + columns] = source[
                rows_ref[k], first : first + count, :
            ]

    shapes = [jax.ShapeDtypeStruct(shape, gathered.dtype) for shape in outs]
    return layout_call(kernel, shapes, "place", [rows_at], [gathered])


def fold(matrix, columns):
    return jnp.concatenate(jnp.split(matrix, matrix.shape[-1] // columns, axis=-1), axis=-2)


def unfold(matrix, rows):
    return jnp.concatenate(jnp.split(matrix, matrix.shape[-2] // rows, axis=-2), axis=-1)


def local(
    dp,
    seq,
    source_embed,
    target_embed,
    source_docs,
    target_docs,
    label_index,
    label_token,
    attend_in,
    attend_out,
    feed_up,
    feed_down,
    norm_gain,
    norm_bias,
    vocab_table,
):
    micro, unused, tokens, width = source_embed.shape
    labels = label_index.shape[2]
    norms, share = norm_gain.shape
    hidden_share = feed_down.shape[1]
    grid = Grid(dp, seq)
    grid.here()
    R, I, G, K, n = grid.R, grid.I, grid.G, grid.K, grid.n
    part = width // G
    hid = hidden_share * K

    def to_row(embed):
        got = []
        for k in range(micro):
            message = jnp.where((grid.b ^ k) == 0, embed[0, 0], embed[1, 0])
            got.append(grid.send(message, lambda r, c, a, i, b: (r, a, b ^ k, i, c)))
        return jnp.where(grid.a == 0, jnp.concatenate(got), jnp.concatenate(got[::-1])).astype(F32)

    def from_row(gradient):
        gradient = gradient.astype(BF16)
        got = []
        for k in range(micro):
            message = jnp.where((grid.a ^ k) == 0, gradient[:tokens], gradient[tokens:])
            got.append(grid.send(message, lambda r, c, a, i, b: (r, b, c, i, a ^ k)))
        return jnp.where(grid.b == 0, jnp.stack(got), jnp.stack(got[::-1])).astype(F32)[:, None]

    kernels = share % 16 == 0 and hidden_share % 16 == 0 and part % LANES == 0

    def member_rows(k, member):
        return grid.flat(k // 4, member // I, k // 2 % 2, member % I, k % 2) * share

    def natural_in(found):
        gathered, rows_at = found
        if not kernels:
            gathered = jnp.take(gathered, rows_at, axis=0).reshape(R, 2, 2, 2, I, 3, share, part)
            return gathered.transpose(0, 3, 1, 4, 2, 6, 5, 7).reshape(width, 3 * part)
        moves = [
            (0, member_rows(k, member), j * part, k, (member * 3 + j) * share, share)
            for k in range(K)
            for member in range(G)
            for j in range(3)
        ]
        return place(gathered, rows_at, [(width, 3 * part)], moves)[0]

    def natural_out(found):
        gathered, rows_at = found
        if not kernels:
            gathered = jnp.take(gathered, rows_at, axis=0)
            return [
                gathered[:, i * share : (i + 1) * share].reshape(part, width) for i in range(3)
            ]
        moves = [(i, k * share, 0, k, i * share, share) for k in range(K) for i in range(3)]
        return place(gathered, rows_at, [(part, width)] * 3, moves)

    def out_home(block):
        member, row = block // K, block % K
        return (row // 4, member // I, row // 2 % 2, member % I, row % 2)

    def in_blocks(weight):
        return weight.reshape(-1, G, part).transpose(1, 0, 2)

    first = grid.exchange(in_blocks(attend_in[0].reshape(3 * share, width)))
    in_0 = Gathering(grid, first.reshape(-1, part), "abr")
    in_0.step()
    source = to_row(source_embed)

    small = jnp.concatenate(
        [
            a.astype(F32).reshape(-1)
            for a in (
                norm_gain,
                norm_bias,
                source_docs,
                target_docs,
                label_index,
                label_token,
            )
        ]
    )
    small = grid.everyone(small)
    edges = [0]
    for length in (norms * share, norms * share, micro * tokens, micro * tokens):
        edges.append(edges[-1] + length)
    for length in (micro * labels, micro * labels):
        edges.append(edges[-1] + length)
    pieces = [small[:, edges[i] : edges[i + 1]] for i in range(6)]
    rows = small[:, : edges[2]].reshape(n, 2 * norms, share).transpose(1, 0, 2)
    rows = lax.optimization_barrier(rows.reshape(2 * norms, width))
    gains, biases = rows[:norms], rows[norms:]

    def row_of(piece, length):
        whole = piece.reshape(R, 2, 2, I, 2, micro, length)
        whole = lax.dynamic_index_in_dim(whole, grid.r, 0, False)
        whole = lax.dynamic_index_in_dim(whole, grid.b, 0, False)
        return lax.dynamic_index_in_dim(whole, grid.a, 3, False)

    def row_order(values):
        values = values.transpose(1, 0, 2, 3)
        values = jnp.where(grid.c == 0, values, values[:, ::-1])
        shifted = values
        for shift in range(1, I):
            shifted = jnp.where(grid.i == shift, jnp.roll(values, -shift, axis=0), shifted)
        return shifted.reshape(-1)

    source_row_docs = row_order(row_of(pieces[2], tokens)).astype(jnp.int32)
    target_row_docs = row_order(row_of(pieces[3], tokens)).astype(jnp.int32)
    places = row_order(jnp.arange(4 * I * tokens, dtype=jnp.int32).reshape(2, I, 2, tokens))
    own_index = lax.dynamic_index_in_dim(row_of(pieces[4], labels), grid.c, 0, False)
    own_index = lax.dynamic_index_in_dim(own_index, grid.i, 0, False).astype(jnp.int32)
    slots = jnp.arange(2)[:, None]
    label_rows = (
        own_index - ((grid.c * I + grid.i) * 2 + slots) * tokens + slots * tokens
    ).reshape(-1)
    own_labels = 2 * labels
    every_token = (
        pieces[5]
        .reshape(R, 2, 2, I, 2, micro, labels)
        .transpose(0, 2, 5, 3, 1, 4, 6)
        .reshape(n, own_labels)
        .astype(jnp.int32)
    )

    later_in, feed_up, target_embed, attend_out, unused = lax.optimization_barrier(
        (attend_in[1:], feed_up, target_embed, attend_out, in_0.gathered)
    )
    out_piece = grid.send(
        attend_out, lambda r, c, a, i, b: out_home(grid.flat(r, c, a, i, b))
    ).reshape(3 * share, width)
    ups = feed_up.reshape(2 * share, R, 2, 2, I, 2, hidden_share)
    ups = grid.exchange(ups.transpose(2, 4, 0, 1, 3, 5, 6).reshape(G, 2 * share, hid))
    later_in = grid.exchange(in_blocks(later_in.reshape(6 * share, width)))
    target = to_row(target_embed)

    def in_bundle(which):
        return later_in[:, (which - 1) * 3 * share : which * 3 * share].reshape(-1, part)

    def feed_bundle(which):
        up = ups[:, which * share : (which + 1) * share].reshape(-1, hid)
        return jnp.concatenate([up, fold(feed_down[which], hid)])

    def feed_weights(found):
        gathered, rows_at = found
        folds = width // hid
        if not kernels:
            gathered = jnp.take(gathered, rows_at, axis=0)
            up = gathered[:, : G * share].reshape(R, 2, 2, 2, I, share, hid)
            down = unfold(gathered[:, G * share :], hidden_share)
            return up.transpose(0, 3, 1, 4, 2, 5, 6).reshape(width, hid), down.reshape(hid, width)
        moves = [
            (0, member_rows(k, member), 0, k, member * share, share)
            for k in range(K)
            for member in range(G)
        ]
        for k in range(K):
            for j in range(folds):
                row = G * share + j * hidden_share
                moves.append((1, k * hidden_share, j * hid, k, row, hidden_share))
        return place(gathered, rows_at, [(width, hid), (hid, width)], moves)

    def meta(query_docs, key_docs):
        return (key_docs[:, None], query_docs[None, :], places[:, None], places[None, :])

    source_meta = meta(source_row_docs, source_row_docs)
    target_meta = meta(target_row_docs, target_row_docs)
    cross_meta = meta(target_row_docs, source_row_docs)
    chip = 4 * tokens
    rows = I * chip

    order = Order()

    def launch(own):
        return own, grid.far_chips(own)

    def apply_near(launched, apply):
        chip_rows = order.use(grid.both_cores(launched[0]))
        return chip_rows, order.did(apply(chip_rows, 0))

    def apply_far(launched, apply):
        chips, results = [], []
        for k, array in enumerate(launched[1]):
            chips.append(order.use(grid.both_cores(order.use(array))))
            results.append(order.did(apply(chips[-1], k + 1)))
        return chips, results

    def apply_all(launched, apply):
        near, near_result = apply_near(launched, apply)
        chips, results = apply_far(launched, apply)
        return [near] + chips, [near_result] + results

    def send_far(parts):
        joints = [order.did(grid.join_cores(array)) for array in parts]
        return [grid.return_chip(joint, k + 1) for k, joint in enumerate(joints)]

    def receive(near_part, sent):
        total = grid.join_cores(near_part)
        for array in sent:
            total = total + order.use(array).astype(F32)
        return total

    def attend_far(arrays, offsets, meta_rows, causal):
        held = order.use(arrays[0])
        arrays = [held if array is arrays[0] else array for array in arrays]
        far = attend_call(arrays, offsets, meta_rows, causal, part, chip, rows - chip)
        order.did(far[0])
        return far

    def attend_near(arrays, offsets, meta_rows, causal):
        held = order.use(arrays[0])
        arrays = [held if array is arrays[0] else array for array in arrays]
        near = attend_call(arrays, offsets, meta_rows, causal, part, 0, chip)
        order.did(near[0])
        return near

    def by_far_chip(array):
        return [array[k * chip : (k + 1) * chip] for k in range(I - 1)]

    def stored(near, far):
        return [near[0]] + by_far_chip(far[0]), jnp.concatenate([near[1], far[1]], axis=2)

    def far_product(array, weight):
        return [product(order.use(p), weight) for p in by_far_chip(array)]

    def projection(weight):
        return lambda array, unused: product(array, weight).astype(BF16)

    def rise(weight):
        def apply(normed, unused):
            up = product(normed, weight)
            return (up * gelu_gate(up)).astype(BF16)

        return apply

    self_offsets = (0, part, 2 * part)
    cross_offsets = (0, 0, part)

    out_all = Gathering(grid, out_piece, "arb")
    feed_0 = Gathering(grid, feed_bundle(0), "abr")
    in_1 = Gathering(grid, in_bundle(1), "arb")
    in_2 = Gathering(grid, in_bundle(2), "abr")
    feed_1 = Gathering(grid, feed_bundle(1), "arb")

    enc_start = layer_norm(source, gains[0], biases[0])
    enc_normed = layer_norm(enc_start, gains[1], biases[1]).astype(BF16)
    in_0.step()
    out_all.step(in_0.gathered)
    in_0.step()
    enc_launched = launch(enc_normed)
    dec_start = layer_norm(target, gains[4], biases[4])
    dec_normed = layer_norm(dec_start, gains[5], biases[5]).astype(BF16)
    feed_0.step(out_all.gathered)
    out_all.step(in_0.gathered)
    in_1.step(in_0.gathered)
    w_in_0 = order.did(natural_in(in_0.finish(dec_normed)))
    enc_in, results = apply_all(enc_launched, projection(w_in_0))
    enc_qkv = jnp.concatenate(results)
    in_1.step(order.last)
    feed_0.step(order.last)
    out_all.step(order.last)
    enc_source = ([enc_qkv] * 3, self_offsets, source_meta, False)
    far = attend_far(*enc_source)
    near = attend_near(*enc_source)
    feed_0.step(order.last)
    in_1.step(order.last)
    dec_launched = launch(dec_normed)
    w_out = natural_out(out_all.finish(order.last))
    enc_mixed, enc_log = stored(near, far)
    sent = send_far(far_product(far[0], w_out[0]))
    in_2.step(order.last)
    near_part = product(order.use(near[0]), w_out[0])
    w_in_1 = order.did(natural_in(in_1.finish(order.last)))
    dec_in, results = apply_all(dec_launched, projection(w_in_1))
    dec_qkv = jnp.concatenate(results)
    enc_middle = order.did(enc_start + receive(near_part, sent))
    ff_normed = layer_norm(enc_middle, gains[2], biases[2]).astype(BF16)
    enc_launched = launch(order.did(ff_normed))
    in_2.step(order.last)
    feed_1.step(order.last)
    dec_source = ([dec_qkv] * 3, self_offsets, target_meta, True)
    far = attend_far(*dec_source)
    sent = send_far(far_product(far[0], w_out[1]))
    near = attend_near(*dec_source)
    dec_mixed, dec_log = stored(near, far)
    near_part = product(near[0], w_out[1])
    up_0, down_0 = feed_weights(feed_0.finish(near_part))
    feed_1.step(near_part)
    in_2.step(near_part)
    dec_self = order.did(dec_start + receive(near_part, sent))
    cross_normed = layer_norm(dec_self, gains[6], biases[6]).astype(BF16)
    ff_chips_0, hidden_0 = apply_all(enc_launched, rise(up_0))
    sent = send_far([product(h, down_0) for h in hidden_0[1:]])
    cross_launched = launch(cross_normed)
    enc_end = enc_middle + receive(product(order.use(hidden_0[0]), down_0), sent)
    encoded = order.did(layer_norm(enc_end, gains[3], biases[3]).astype(BF16))
    encoded_launched = launch(encoded)
    w_in_2 = natural_in(in_2.finish(order.last))
    cross_w_q, cross_w_kv = w_in_2[:, :part], w_in_2[:, part:]
    cross_in, results = apply_all(cross_launched, projection(cross_w_q))
    cross_q = jnp.concatenate(results)
    encoded_in, results = apply_all(encoded_launched, projection(cross_w_kv))
    cross_kv = jnp.concatenate(results)
    cross_source = ([cross_q, cross_kv, cross_kv], cross_offsets, cross_meta, False)
    feed_1.step(order.last)
    far = attend_far(*cross_source)
    sent = send_far(far_product(far[0], w_out[2]))
    near = attend_near(*cross_source)
    cross_mixed, cross_log = stored(near, far)
    dec_cross = dec_self + receive(product(near[0], w_out[2]), sent)
    ff_normed = order.did(layer_norm(dec_cross, gains[7], biases[7]).astype(BF16))
    dec_launched = launch(ff_normed)
    up_1, down_1 = feed_weights(feed_1.finish(order.last))
    ff_chips_1, hidden_1 = apply_all(dec_launched, rise(up_1))
    sent = send_far([product(h, down_1) for h in hidden_1[1:]])
    dec_end = dec_cross + receive(product(order.use(hidden_1[0]), down_1), sent)
    final = order.did(layer_norm(dec_end, gains[8], biases[8]))

    all_rows = grid.everyone(jnp.take(final, label_rows, axis=0).astype(BF16))
    all_rows = all_rows.reshape(n * own_labels, width)
    every_token = every_token.reshape(-1)
    vocab_rows = vocab_table.shape[0]
    vocab_places = grid.me * vocab_rows + jnp.arange(vocab_rows, dtype=jnp.int32)
    logits = by_transpose(all_rows, vocab_table)
    target_hit = every_token[:, None] == vocab_places[None, :]
    row_max = jnp.max(logits, axis=-1)
    stats = jnp.stack(
        [
            row_max,
            jnp.sum(jnp.exp(logits - row_max[:, None]), axis=-1),
            jnp.sum(jnp.where(target_hit, logits, 0.0), axis=-1),
        ]
    )
    every_stats = grid.everyone(stats)
    joint = jnp.max(every_stats[:, 0], axis=0)
    total = jnp.sum(every_stats[:, 1] * jnp.exp(every_stats[:, 0] - joint), axis=0)
    stats = (joint, total, jnp.sum(every_stats[:, 2], axis=0))
    log_total = stats[0] + jnp.log(stats[1])
    mean_loss = jnp.sum(log_total - stats[2]) / (n * own_labels)
    grad_logits = (jnp.exp(logits - log_total[:, None]) - target_hit.astype(F32)).astype(BF16)
    grad_rows = product(grad_logits, vocab_table).reshape(n, own_labels, width)
    table_grad = rows_inner(grad_logits, all_rows)
    grad_rows = lax.all_to_all(grad_rows.astype(BF16), AXES, 0, 0)
    grad_rows = jnp.sum(grad_rows.astype(F32), axis=0)
    grad_final = jnp.zeros(final.shape, F32).at[label_rows].add(grad_rows)

    gain_grads = [None] * norms
    bias_grads = [None] * norms

    def back_norm(values, norm, gradient):
        result, gain_grads[norm], bias_grads[norm] = norm_back(values, gains[norm], gradient)
        return result

    def rows_sum(left, right):
        left, right = (
            order.use(a if not isinstance(a, list) else jnp.concatenate(a)) for a in (left, right)
        )
        return order.did(rows_inner(left, right).astype(BF16))

    def far_back(grads, weight):
        return send_far([by_transpose(order.use(g), weight) for g in grads[1:]])

    def near_back(grads, weight):
        return order.did(by_transpose(order.use(grads[0]), weight))

    def fall(chips, up_weight, down_weight):
        def apply(grad, k):
            up = product(chips[k], up_weight)
            return (by_transpose(grad, down_weight) * gelu_slope(up)).astype(BF16)

        return apply

    def back_projection(weight):
        return lambda grad, unused: by_transpose(grad, weight).astype(BF16)

    def attend_back(source, log_total, grad_mixed):
        arrays, offsets, meta_rows, causal = source
        grad_mixed = order.use(jnp.concatenate(grad_mixed))
        return order.did(
            attend_back_call(arrays, offsets, meta_rows, causal, part, log_total, grad_mixed)
        )

    def by_chip(matrix):
        return [matrix[i * chip : (i + 1) * chip] for i in range(I)]

    def feed_scatter(up_grad, down_grad, name):
        up_grad = up_grad.reshape(R, 2, 2, I, 2, share, hid)
        up_grad = up_grad.transpose(0, 2, 4, 1, 3, 5, 6).reshape(R, 2, 2, G * share, hid)
        down_grad = fold(down_grad.reshape(R, 2, 2, hidden_share, width), hid)
        bundle = jnp.concatenate([up_grad, down_grad], axis=3)
        return Scattering(grid, bundle, name, (0, 1, 2))

    def settle_feed(total):
        total = total[0, 0, 0]
        up = grid.exchange(total[: G * share].reshape(G, share, hid).astype(BF16))
        up = up.reshape(2, I, share, R, 2, 2, hidden_share).transpose(2, 3, 0, 4, 1, 5, 6)
        return up.reshape(share, -1).astype(F32), unfold(total[G * share :], hidden_share)

    def in_scatter(grads, name):
        grads = grads.reshape(R, 2, 2, I, 2, share, 3 * part)
        return Scattering(grid, grads, name, (0, 2, 4))

    def settle_in(total):
        total = grid.exchange(total.reshape(G, share, 3 * part).astype(BF16)).astype(F32)
        return total.reshape(G, share, 3, part).transpose(2, 1, 0, 3).reshape(3, share, width)

    grad_dec_end = back_norm(dec_end, 8, grad_final)
    launched = launch(order.did(grad_dec_end.astype(BF16)))
    branch, grad_ups = apply_all(launched, fall(ff_chips_1, up_1, down_1))
    sent = far_back(grad_ups, up_1)
    near_part = near_back(grad_ups, up_1)
    feed_1 = feed_scatter(
        rows_sum(ff_chips_1, grad_ups), rows_sum(hidden_1, branch), "abr"
    )
    feed_1.step(order.last)
    grad_dec_cross = grad_dec_end + back_norm(dec_cross, 7, receive(near_part, sent))

    launched = launch(order.did(grad_dec_cross.astype(BF16)))
    branch, grad_mixed = apply_all(launched, back_projection(w_out[2]))
    grads = attend_back(cross_source, cross_log, grad_mixed)
    grad_q, grad_kv = grads[:, :part], grads[:, part:]
    sent_kv = far_back(by_chip(grad_kv), cross_w_kv)
    sent_q = far_back(by_chip(grad_q), cross_w_q)
    near_kv = near_back(by_chip(grad_kv), cross_w_kv)
    near_q = near_back(by_chip(grad_q), cross_w_q)
    out_2 = rows_sum(cross_mixed, branch)
    grad_enc_end = back_norm(enc_end, 3, receive(near_kv, sent_kv))
    enc_launched = launch(order.did(grad_enc_end.astype(BF16)))
    in_grad_q = rows_sum(cross_in, grad_q)
    in_grad_kv = rows_sum(encoded_in, grad_kv)
    in_2 = in_scatter(jnp.concatenate([in_grad_q, in_grad_kv], axis=1), "arb")
    in_2.step(order.last)
    grad_dec_self = grad_dec_cross + back_norm(dec_self, 6, receive(near_q, sent_q))
    dec_launched = launch(order.did(grad_dec_self.astype(BF16)))
    feed_1.step(order.last)

    enc_branch, grad_ups = apply_all(enc_launched, fall(ff_chips_0, up_0, down_0))
    sent = far_back(grad_ups, up_0)
    near_part = near_back(grad_ups, up_0)
    feed_0 = feed_scatter(
        rows_sum(ff_chips_0, grad_ups), rows_sum(hidden_0, enc_branch), "abr"
    )
    feed_0.step(order.last)
    in_2.step(order.last)
    grad_enc_middle = grad_enc_end + back_norm(enc_middle, 2, receive(near_part, sent))
    enc_launched = launch(order.did(grad_enc_middle.astype(BF16)))
    feed_1.step(order.last)
    dec_branch, grad_mixed = apply_all(dec_launched, back_projection(w_out[1]))
    grads_1 = attend_back(dec_source, dec_log, grad_mixed)
    in_2.step(order.last)

    branch, grad_mixed = apply_all(enc_launched, back_projection(w_out[0]))
    sent_1 = far_back(by_chip(grads_1), w_in_1)
    grads_0 = attend_back(enc_source, enc_log, grad_mixed)
    sent_0 = far_back(by_chip(grads_0), w_in_0)
    near_0 = near_back(by_chip(grads_0), w_in_0)
    near_1 = near_back(by_chip(grads_1), w_in_1)
    feed_0.step(order.last)
    in_0 = in_scatter(rows_sum(enc_in, grads_0), "arb")
    in_0.step(order.last)
    in_1 = in_scatter(rows_sum(dec_in, grads_1), "abr")
    in_1.step(order.last)
    grad_enc_start = grad_enc_middle + back_norm(enc_start, 1, receive(near_0, sent_0))
    source_grad = from_row(order.did(back_norm(source, 0, grad_enc_start)))
    grad_dec_start = grad_dec_self + back_norm(dec_start, 5, receive(near_1, sent_1))
    target_grad = from_row(order.did(back_norm(target, 4, grad_dec_start)))
    outs = [rows_sum(enc_mixed, branch), rows_sum(dec_mixed, dec_branch), out_2]
    out_grads = jnp.concatenate([g.reshape(R, 2, 2, share, width) for g in outs], axis=3)
    out_all = Scattering(grid, out_grads, "abr", (0, 1, 2))
    out_all.step(order.last)
    feed_0.step(order.last)
    in_0.step(order.last)
    in_1.step(order.last)

    def out_owner(r, c, a, i, b):
        block = (c * I + i) * K + (r * 2 + a) * 2 + b
        return (
            block // (8 * I),
            block // (4 * I) % 2,
            block // (2 * I) % 2,
            block // 2 % I,
            block % 2,
        )

    feed_1 = settle_feed(feed_1.finish())
    in_2 = settle_in(in_2.finish())
    in_1 = settle_in(in_1.finish())
    feed_0 = settle_feed(feed_0.finish())
    attend_out_grad = grid.send(out_all.finish().reshape(3, share, width), out_owner)
    in_0 = settle_in(in_0.finish())

    norm_grads = jnp.stack(gain_grads + bias_grads)
    norm_grads = norm_grads.reshape(2 * norms, n, share).transpose(1, 0, 2)
    norm_grads = jnp.sum(lax.all_to_all(norm_grads, AXES, 0, 0), axis=0)

    return (
        mean_loss,
        source_grad,
        target_grad,
        jnp.stack([in_0, in_1, in_2]),
        attend_out_grad,
        jnp.stack([feed_0[0], feed_1[0]]),
        jnp.stack([feed_0[1], feed_1[1]]),
        norm_grads[:norms],
        norm_grads[norms:],
        table_grad,
    )


def solution(mesh):
    dp, seq = mesh.shape["dp"], mesh.shape["seq"]
    mesh = jax.sharding.Mesh(mesh.devices.reshape(dp // 2, 2, 2, seq // 4, 2), AXES)

    def placed_local(*arrays):
        return local(dp, seq, *arrays)

    rows = P(None, ("r", "c"), ("a", "i", "b"), None)
    flat = P(None, ("r", "c"), ("a", "i", "b"))
    weight = P(None, AXES, None)
    weight_in = P(None, None, AXES, None)
    norm = P(None, AXES)
    table = P(AXES, None)
    return jax.shard_map(
        placed_local,
        mesh=mesh,
        in_specs=(
            (rows, rows, flat, flat, flat, flat)
            + (weight_in, weight, weight, weight, norm, norm, table)
        ),
        out_specs=(P(), rows, rows, weight_in, weight, weight, weight, norm, norm, table),
        check_vma=False,
    )
```

```python
import functools
import math

import jax
import jax.numpy as jnp
from jax import lax
from jax.experimental import pallas as pl
from jax.experimental.pallas import tpu as pltpu
from jax.sharding import PartitionSpec as P

HEADS = 16
HEAD = 64

EPSILON = 1e-05
MASK_VALUE = -1000000000.0
AXES = ("r", "c", "a", "i", "b")
MEMBERS = ("c", "i")
ACROSS = ("r", "a", "b")
BF16 = jnp.bfloat16
F32 = jnp.float32


def product(left, right):
    return jnp.dot(left, right, preferred_element_type=F32)


def by_transpose(left, right):
    return lax.dot_general(left, right, (((1,), (1,)), ((), ())), preferred_element_type=F32)


def rows_inner(left, right):
    return lax.dot_general(left, right, (((0,), (0,)), ((), ())), preferred_element_type=F32)


def tie(value, *others):
    return lax.optimization_barrier((value,) + others)[0]


def gate_kernel(*refs):
    pass


def gate(value, *others):
    anywhere = pl.BlockSpec(memory_space=pl.ANY)
    return pl.pallas_call(
        gate_kernel,
        in_specs=[anywhere] * (1 + len(others)),
        out_specs=anywhere,
        out_shape=jax.ShapeDtypeStruct(value.shape, value.dtype),
        input_output_aliases={0: 0},
        cost_estimate=pl.CostEstimate(flops=int(6e10), bytes_accessed=0, transcendentals=0),
        name="gate",
    )(value, *others)


def without(kernel, first, count):
    return lambda *refs: kernel(*refs[:first], *refs[first + count :])


class Grid:
    def __init__(self, dp, seq):
        self.R, self.C, self.A, self.B = dp // 2, 2, 2, 2
        self.I = seq // 4
        self.n = dp * seq
        self.G = self.C * self.I
        self.K = self.R * self.A * self.B

    def flat(self, r, c, a, i, b):
        return (((r * 2 + c) * 2 + a) * self.I + i) * 2 + b

    def here(self):
        me = lax.axis_index(AXES)
        self.me = me
        self.b = me % 2
        self.i = (me // 2) % self.I
        self.a = (me // (2 * self.I)) % 2
        self.c = (me // (4 * self.I)) % 2
        self.r = me // (8 * self.I)

    def send(self, array, move):
        pairs = []
        for r in range(self.R):
            for c in range(2):
                for a in range(2):
                    for i in range(self.I):
                        for b in range(2):
                            pairs.append(
                                (self.flat(r, c, a, i, b), self.flat(*move(r, c, a, i, b)))
                            )
        return lax.ppermute(array, AXES, pairs)

    def everyone(self, row):
        return lax.all_to_all(jnp.broadcast_to(row[None], (self.n,) + row.shape), AXES, 0, 0)

    def phases(self):
        size = self.I
        core = 4 * size
        others = [1 << k for k in range(int(math.log2(self.n))) if 1 << k != core]
        near = [bit for bit in others if bit < 2 * size]
        groups, rest = [], [bit for bit in others if bit not in near]
        while rest:
            groups.append(rest[:2])
            rest = rest[2:]
        return groups + [near[k : k + 2] for k in range(0, len(near), 2)] + [[core]]

    def flips(self, group):
        found = [0]
        for bit in group:
            found = found + [bit ^ other for other in found]
        return found[1:]

    def flip(self, array, mask):
        return lax.ppermute(array, AXES, [(d, d ^ mask) for d in range(self.n)])

    def spread(self, rows):
        rows, holders = rows[None], [0]
        for group in self.phases():
            masks = self.flips(group)
            rows = jnp.concatenate([rows] + [self.flip(rows, mask) for mask in masks])
            holders = holders + [holder ^ mask for mask in masks for holder in holders]
        return rows, holders

    def collect(self, parts):
        for group in reversed(self.phases()):
            masks = self.flips(group)
            count = parts.shape[0] // (len(masks) + 1)
            total = parts[:count]
            for k, mask in enumerate(masks):
                piece = parts[(k + 1) * count : (k + 2) * count].astype(BF16)
                total = total + self.flip(piece, mask).astype(F32)
            parts = total
        return parts[0]

    def swap_cores(self, array):
        return self.send(array, lambda r, c, a, i, b: (r, 1 - c, a, i, b))

    def far_chips(self, own):
        return [
            self.send(own, lambda r, c, a, i, b: (r, c, a, (i - di) % self.I, b))
            for di in range(1, self.I)
        ]

    def both_cores(self, array):
        return jnp.concatenate([array, self.swap_cores(array)])

    def join_cores(self, part):
        half = part.shape[0] // 2
        return part[:half] + self.swap_cores(part[half:].astype(BF16)).astype(F32)

    def return_chip(self, joint, di):
        return self.send(
            joint.astype(BF16), lambda r, c, a, i, b: (r, c, a, (i + di) % self.I, b)
        )

    def exchange(self, blocks):
        return lax.all_to_all(blocks, MEMBERS, 0, 0)

    def steps(self, order):
        found = []
        for name in order:
            if name == "a":
                found.append((1, 0, self.a, lambda r, c, a, i, b: (r, c, 1 - a, i, b)))
            elif name == "b":
                found.append((2, 0, self.b, lambda r, c, a, i, b: (r, c, a, i, 1 - b)))
            else:
                for bit in range(int(math.log2(self.R))):
                    found.append(
                        (
                            0,
                            bit,
                            (self.r >> bit) & 1,
                            lambda r, c, a, i, b, bit=bit: (r ^ (1 << bit), c, a, i, b),
                        )
                    )
        return found


class Gathering:
    def __init__(self, grid, piece, order):
        self.grid, self.gathered, self.got = grid, piece[None], None
        self.moves = grid.steps(order)
        self.places = [(0, 0, 0)]

    def land(self, after):
        if self.got is not None:
            self.gathered = jnp.concatenate([self.gathered, self.got])
            self.got = None

    def step(self, *after):
        self.land(after)
        axis, bit, unused, move = self.moves.pop(0)
        self.got = self.grid.send(self.gathered, move)
        moved = tuple((1 << bit) if axis == j else 0 for j in range(3))
        self.places = self.places + [
            tuple(p ^ q for p, q in zip(place, moved)) for place in self.places
        ]
        return self.gathered

    def finish(self, *after):
        while self.moves:
            self.step(*after)
        self.land(after)
        grid, found_at = self.grid, []
        for r in range(grid.R):
            for a in range(2):
                for b in range(2):
                    index = 0
                    for k, (pr, pa, pb) in enumerate(self.places):
                        found = ((grid.r ^ pr) == r) & ((grid.a ^ pa) == a) & ((grid.b ^ pb) == b)
                        index = index + jnp.where(found, k, 0)
                    found_at.append(index)
        return self.gathered, jnp.stack(found_at).astype(jnp.int32)


class Scattering:
    def __init__(self, grid, parts, order, axes):
        self.grid, self.parts, self.got = grid, parts, None
        self.moves = [
            (axes[axis], up, move) for axis, bit, up, move in reversed(grid.steps(order))
        ]

    def land(self, after):
        if self.got is not None:
            self.parts = self.keep.astype(F32) + self.got.astype(F32)
            self.got = None

    def step(self, *after):
        self.land(after)
        axis, up, move = self.moves.pop(0)
        half = self.parts.shape[axis] // 2
        self.keep = lax.dynamic_slice_in_dim(self.parts, up * half, half, axis)
        give = lax.dynamic_slice_in_dim(self.parts, (1 - up) * half, half, axis).astype(BF16)
        self.got = self.grid.send(give, move)
        return give

    def finish(self, *after):
        while self.moves:
            self.step(*after)
        self.land(after)
        return self.parts


class Order:
    def __init__(self):
        self.last = None
        self.kept = False

    def use(self, value):
        return value if self.last is None else tie(value, self.last)

    def did(self, value):
        if self.kept:
            self.last = value
        return value


def normalized(values):
    center = jnp.mean(values, axis=-1, keepdims=True)
    shifted = values - center
    spread = jnp.mean(shifted * shifted, axis=-1, keepdims=True)
    rate = lax.rsqrt(spread + EPSILON)
    return shifted * rate, rate


def layer_norm(values, gain, bias):
    unit, rate = normalized(values)
    return unit * gain + bias


def norm_back(values, gain, gradient):
    unit, rate = normalized(values)
    scaled = gradient * gain
    mean_grad = jnp.mean(scaled, axis=-1, keepdims=True)
    mean_along = jnp.mean(scaled * unit, axis=-1, keepdims=True)
    return (
        rate * (scaled - mean_grad - unit * mean_along),
        jnp.sum(gradient * unit, axis=0),
        jnp.sum(gradient, axis=0),
    )


def gelu_gate(values):
    return 0.5 + 0.5 * lax.erf(values * math.sqrt(0.5))


def gelu_slope(values):
    density = jnp.exp(-0.5 * values * values) * (1.0 / math.sqrt(2.0 * math.pi))
    return gelu_gate(values) + values * density


LANES = 128
DOCUMENTS = 3
SCALE = 1.0 / math.sqrt(HEAD)


def in_head(values, head):
    lane = lax.broadcasted_iota(jnp.int32, values.shape, 1)
    inside = (lane >= head * HEAD) & (lane < (head + 1) * HEAD)
    return jnp.where(inside, values, jnp.zeros_like(values))


def inner(left, right, left_dim, right_dim):
    return lax.dot_general(
        left, right, (((left_dim,), (right_dim,)), ((), ())), preferred_element_type=F32
    )


def head_rows(values, head):
    row = lax.broadcasted_iota(jnp.int32, values.shape, 0)
    inside = (row >= head * HEAD) & (row < (head + 1) * HEAD)
    return jnp.where(inside, values, jnp.zeros_like(values))


def turned(values):
    return jnp.transpose(values.astype(F32)).astype(values.dtype)


def doc_lanes(docs, head):
    spare = HEAD if head == 0 else 0
    lane = lax.broadcasted_iota(jnp.int32, (docs.shape[0], LANES), 1)
    return lane - spare == docs, (lane >= spare) & (lane < spare + DOCUMENTS)


def marked_keys(keys, docs, head):
    own, any_doc = doc_lanes(docs, head)
    marks = jnp.where(any_doc & jnp.logical_not(own), MASK_VALUE, 0.0).astype(BF16)
    return in_head(keys, head) + marks


def marked_queries(queries, docs, head):
    own, unused = doc_lanes(docs, head)
    return in_head(queries, head) + jnp.where(own, 1.0, 0.0).astype(BF16)


def blocked(rows):
    size = min(rows, 1024)
    return [slice(start, start + size) for start in range(0, rows, size)]


def attend_kernel(
    causal,
    q,
    k,
    v,
    key_docs,
    query_docs,
    key_places,
    query_places,
    mixed,
    exact,
    log_total,
    v_turned,
    marked,
):
    heads = LANES // HEAD

    @pl.when(pl.program_id(1) == 0)
    def prepare():
        v_turned[...] = turned(v[...])
        for head in range(heads):
            marked[head] = marked_keys(k[...], key_docs[...], head)

    queries = q[...] * jnp.asarray(SCALE, BF16)
    result = None
    for head in range(heads):
        head_queries = marked_queries(queries, query_docs[...], head)
        row_max, row_sum, total = None, None, None
        for rows in blocked(k.shape[0]):
            scores = inner(marked[head, rows, :], head_queries, 1, 1)
            if causal:
                scores = jnp.where(key_places[rows, :] <= query_places[...], scores, MASK_VALUE)
            block_max = jnp.max(scores, axis=0, keepdims=True)
            new_max = block_max if row_max is None else jnp.maximum(row_max, block_max)
            exponent = jnp.exp(scores - new_max)
            block_sum = jnp.sum(exponent, axis=0, keepdims=True)
            block = inner(v_turned[:, rows], exponent.astype(BF16), 1, 0)
            if row_max is None:
                row_sum, total = block_sum, block
            else:
                decay = jnp.exp(row_max - new_max)
                row_sum, total = row_sum * decay + block_sum, total * decay + block
            row_max = new_max
        part = head_rows(total * (1.0 / row_sum), head)
        result = part if result is None else result + part
        log_total[0, head : head + 1, :] = row_max + jnp.log(row_sum)
    result = jnp.transpose(result)
    exact[...] = result
    mixed[...] = result.astype(BF16)


def attend_back_kernel(
    causal,
    q,
    k,
    v,
    key_docs,
    query_docs,
    key_places,
    query_places,
    log_total,
    grad_mixed,
    exact,
    grads,
    grad_keys,
    grad_values,
    k_turned,
    marked,
):
    pair, tile = pl.program_id(0), pl.program_id(1)
    pairs, tiles = pl.num_programs(0), pl.num_programs(1)
    size = q.shape[0]
    heads = LANES // HEAD

    @pl.when(tile == 0)
    def clear():
        grad_keys[...] = jnp.zeros_like(grad_keys)
        grad_values[...] = jnp.zeros_like(grad_values)
        k_turned[...] = turned(k[...])
        for head in range(heads):
            marked[head] = marked_keys(k[...], key_docs[...], head)

    queries = q[...] * jnp.asarray(SCALE, BF16)
    along = jnp.transpose(grad_mixed[...].astype(F32) * exact[...])
    grad_queries = None
    for head in range(heads):
        head_queries = in_head(queries, head)
        searched = marked_queries(queries, query_docs[...], head)
        head_grad = in_head(grad_mixed[...], head)
        row_delta = jnp.sum(along[head * HEAD : (head + 1) * HEAD], axis=0, keepdims=True)
        row_log = log_total[0, head : head + 1, :]
        total = None
        for rows in blocked(k.shape[0]):
            scores = inner(marked[head, rows, :], searched, 1, 1)
            if causal:
                scores = jnp.where(key_places[rows, :] <= query_places[...], scores, MASK_VALUE)
            attention = jnp.exp(scores - row_log)
            grad_attention = inner(v[rows, :], head_grad, 1, 1)
            grad_scores = (attention * (grad_attention - row_delta)).astype(BF16)
            grad_values[rows, :] += inner(attention.astype(BF16), head_grad, 1, 0)
            grad_keys[rows, :] += inner(grad_scores, head_queries, 1, 0)
            block = inner(k_turned[:, rows], grad_scores, 1, 0)
            total = block if total is None else total + block
        part = head_rows(total, head)
        grad_queries = part if grad_queries is None else grad_queries + part

    def column(block):
        return pl.ds(pl.multiple_of(block * LANES, LANES), LANES)

    grads[pl.ds(pl.multiple_of(tile * size, size), size), column(pair)] = jnp.transpose(
        grad_queries * SCALE
    ).astype(BF16)

    @pl.when(tile == tiles - 1)
    def store():
        grads[:, column(pairs + pair)] = grad_keys[...].astype(BF16)
        grads[:, column(2 * pairs + pair)] = grad_values[...].astype(BF16)


def attend_specs(rows, tile, offsets, first):
    def keys(offset):
        return pl.BlockSpec((rows, LANES), lambda p, i: (0, offset + p))

    row = pl.BlockSpec((1, tile), lambda p, i: (0, first + i))
    column = pl.BlockSpec((rows, 1), lambda p, i: (0, 0))
    docs = pl.BlockSpec((tile, 1), lambda p, i: (first + i, 0))
    return [
        pl.BlockSpec((tile, LANES), lambda p, i: (first + i, offsets[0] + p)),
        keys(offsets[1]),
        keys(offsets[2]),
        column,
        docs,
        column,
        row,
    ]


VMEM_BYTES = 48 * 1024 * 1024


def attend_call(arrays, offsets, meta, causal, part, start, count, early=()):
    rows = arrays[0].shape[0]
    pairs, tile = part // LANES, min(count, 256)
    places = [offset // LANES for offset in offsets]
    return pl.pallas_call(
        without(functools.partial(attend_kernel, causal), 7, len(early)),
        grid=(pairs, count // tile),
        in_specs=attend_specs(rows, tile, places, start // tile)
        + [pl.BlockSpec(memory_space=pl.ANY)] * len(early),
        out_specs=[
            pl.BlockSpec((tile, LANES), lambda p, i: (i, p)),
            pl.BlockSpec((tile, LANES), lambda p, i: (i, p)),
            pl.BlockSpec((1, LANES // HEAD, tile), lambda p, i: (p, 0, i)),
        ],
        out_shape=[
            jax.ShapeDtypeStruct((count, part), BF16),
            jax.ShapeDtypeStruct((count, part), F32),
            jax.ShapeDtypeStruct((pairs, LANES // HEAD, count), F32),
        ],
        scratch_shapes=[
            pltpu.VMEM((LANES, rows), BF16),
            pltpu.VMEM((LANES // HEAD, rows, LANES), BF16),
        ],
        compiler_params=pltpu.CompilerParams(vmem_limit_bytes=VMEM_BYTES),
        cost_estimate=pl.CostEstimate(flops=int(6e10), bytes_accessed=0, transcendentals=0),
        name="attend",
    )(*arrays, *meta, *early)


def attend_back_call(arrays, offsets, meta, causal, part, stored, grad_mixed, early):
    log_total, exact = stored
    rows = arrays[0].shape[0]
    pairs, tile = part // LANES, min(rows, 256)
    places = [offset // LANES for offset in offsets]
    return pl.pallas_call(
        without(functools.partial(attend_back_kernel, causal), 10, len(early)),
        grid=(pairs, rows // tile),
        in_specs=attend_specs(rows, tile, places, 0)
        + [
            pl.BlockSpec((1, LANES // HEAD, tile), lambda p, i: (p, 0, i)),
            pl.BlockSpec((tile, LANES), lambda p, i: (i, p)),
            pl.BlockSpec((tile, LANES), lambda p, i: (i, p)),
        ]
        + [pl.BlockSpec(memory_space=pl.ANY)] * len(early),
        out_specs=pl.BlockSpec((rows, 3 * part), lambda p, i: (0, 0)),
        out_shape=jax.ShapeDtypeStruct((rows, 3 * part), BF16),
        scratch_shapes=[
            pltpu.VMEM((rows, LANES), F32),
            pltpu.VMEM((rows, LANES), F32),
            pltpu.VMEM((LANES, rows), BF16),
            pltpu.VMEM((LANES // HEAD, rows, LANES), BF16),
        ],
        compiler_params=pltpu.CompilerParams(vmem_limit_bytes=VMEM_BYTES),
        cost_estimate=pl.CostEstimate(flops=int(0), bytes_accessed=0, transcendentals=0),
        name="attend_back",
    )(*arrays, *meta, log_total, grad_mixed, exact, *early)


def layout_call(kernel, outs, name, tables, arrays, early):
    whole = pl.BlockSpec(memory_space=pltpu.VMEM)
    return pl.pallas_call(
        kernel,
        grid_spec=pltpu.PrefetchScalarGridSpec(
            num_scalar_prefetch=len(tables),
            grid=(),
            in_specs=[whole] * len(arrays) + [pl.BlockSpec(memory_space=pl.ANY)] * len(early),
            out_specs=[whole] * len(outs),
        ),
        out_shape=outs,
        compiler_params=pltpu.CompilerParams(vmem_limit_bytes=VMEM_BYTES),
        cost_estimate=pl.CostEstimate(flops=int(6e10), bytes_accessed=0, transcendentals=0),
        name=name,
    )(*tables, *arrays, *early)


def place(gathered, rows_at, outs, moves, early=()):
    def kernel(rows_ref, source, *targets):
        targets = targets[len(early) :]
        columns = source.shape[2]
        for out, row, column, k, first, count in moves:
            targets[out][row : row + count, column : column + columns] = source[
                rows_ref[k], first : first + count, :
            ]

    shapes = [jax.ShapeDtypeStruct(shape, gathered.dtype) for shape in outs]
    return layout_call(kernel, shapes, "place", [rows_at], [gathered], early)


def fold(matrix, columns):
    return jnp.concatenate(jnp.split(matrix, matrix.shape[-1] // columns, axis=-1), axis=-2)


def unfold(matrix, rows):
    return jnp.concatenate(jnp.split(matrix, matrix.shape[-2] // rows, axis=-2), axis=-1)


def local(
    dp,
    seq,
    source_embed,
    target_embed,
    source_docs,
    target_docs,
    label_index,
    label_token,
    attend_in,
    attend_out,
    feed_up,
    feed_down,
    norm_gain,
    norm_bias,
    vocab_table,
):
    micro, unused, tokens, width = source_embed.shape
    labels = label_index.shape[2]
    norms, share = norm_gain.shape
    hidden_share = feed_down.shape[1]
    grid = Grid(dp, seq)
    grid.here()
    R, I, G, K, n = grid.R, grid.I, grid.G, grid.K, grid.n
    part = width // G
    hid = hidden_share * K

    def to_row(embed, *early):
        got = []
        for k in range(micro):
            message = jnp.where((grid.b ^ k) == 0, embed[0, 0], embed[1, 0])
            if early:
                message = gate(message, *early)
            got.append(grid.send(message, lambda r, c, a, i, b: (r, a, b ^ k, i, c)))
        return jnp.where(grid.a == 0, jnp.concatenate(got), jnp.concatenate(got[::-1])).astype(F32)

    def from_row(gradient, *early):
        gradient = gradient.astype(BF16)
        if early:
            gradient = gate(gradient, *early)
        got = []
        for k in range(micro):
            message = jnp.where((grid.a ^ k) == 0, gradient[:tokens], gradient[tokens:])
            got.append(grid.send(message, lambda r, c, a, i, b: (r, b, c, i, a ^ k)))
        return jnp.where(grid.b == 0, jnp.stack(got), jnp.stack(got[::-1])).astype(F32)[:, None]

    kernels = share % 16 == 0 and hidden_share % 16 == 0 and part % LANES == 0

    def member_rows(k, member):
        return grid.flat(k // 4, member // I, k // 2 % 2, member % I, k % 2) * share

    def natural_in(found, early=()):
        gathered, rows_at = found
        if not kernels:
            gathered = jnp.take(gathered, rows_at, axis=0)[:, : G * 3 * share]
            gathered = gathered.reshape(R, 2, 2, 2, I, 3, share, part)
            return gathered.transpose(0, 3, 1, 4, 2, 6, 5, 7).reshape(width, 3 * part)
        moves = [
            (0, member_rows(k, member), j * part, k, (member * 3 + j) * share, share)
            for k in range(K)
            for member in range(G)
            for j in range(3)
        ]
        return place(gathered, rows_at, [(width, 3 * part)], moves, early)[0]

    def natural_out(found):
        gathered, rows_at = found
        if not kernels:
            gathered = jnp.take(gathered, rows_at, axis=0)
            return [
                gathered[:, i * share : (i + 1) * share].reshape(part, width) for i in range(3)
            ]
        moves = [(i, k * share, 0, k, i * share, share) for k in range(K) for i in range(3)]
        return place(gathered, rows_at, [(part, width)] * 3, moves)

    def out_home(block):
        member, row = block // K, block % K
        return (row // 4, member // I, row // 2 % 2, member % I, row % 2)

    def in_blocks(weight):
        return weight.reshape(-1, G, part).transpose(1, 0, 2)

    first = in_blocks(attend_in[:2].reshape(6 * share, width))
    source_embed, unused = lax.optimization_barrier((source_embed, first))
    first = grid.exchange(first)
    in_0 = Gathering(grid, first[:, : 3 * share].reshape(-1, part), "abr")
    in_0.step()
    source = to_row(source_embed)
    norm_gain = tie(norm_gain, first)

    small = jnp.concatenate(
        [
            a.astype(F32).reshape(-1)
            for a in (
                norm_gain,
                norm_bias,
                source_docs,
                target_docs,
                label_index,
                label_token,
            )
        ]
    )
    small = grid.everyone(small)
    edges = [0]
    for length in (norms * share, norms * share, micro * tokens, micro * tokens):
        edges.append(edges[-1] + length)
    for length in (micro * labels, micro * labels):
        edges.append(edges[-1] + length)
    pieces = [small[:, edges[i] : edges[i + 1]] for i in range(6)]
    rows = small[:, : edges[2]].reshape(n, 2 * norms, share).transpose(1, 0, 2)
    rows = lax.optimization_barrier(rows.reshape(2 * norms, width))
    gains, biases = rows[:norms], rows[norms:]

    def row_of(piece, length):
        whole = piece.reshape(R, 2, 2, I, 2, micro, length)
        whole = lax.dynamic_index_in_dim(whole, grid.r, 0, False)
        whole = lax.dynamic_index_in_dim(whole, grid.b, 0, False)
        return lax.dynamic_index_in_dim(whole, grid.a, 3, False)

    def row_order(values):
        values = values.transpose(1, 0, 2, 3)
        values = jnp.where(grid.c == 0, values, values[:, ::-1])
        shifted = values
        for shift in range(1, I):
            shifted = jnp.where(grid.i == shift, jnp.roll(values, -shift, axis=0), shifted)
        return shifted.reshape(-1)

    source_row_docs = row_order(row_of(pieces[2], tokens)).astype(jnp.int32)
    target_row_docs = row_order(row_of(pieces[3], tokens)).astype(jnp.int32)
    places = row_order(jnp.arange(4 * I * tokens, dtype=jnp.int32).reshape(2, I, 2, tokens))
    own_index = lax.dynamic_index_in_dim(row_of(pieces[4], labels), grid.c, 0, False)
    own_index = lax.dynamic_index_in_dim(own_index, grid.i, 0, False).astype(jnp.int32)
    slots = jnp.arange(2)[:, None]
    label_rows = (
        own_index - ((grid.c * I + grid.i) * 2 + slots) * tokens + slots * tokens
    ).reshape(-1)
    own_labels = 2 * labels
    every_token = (
        pieces[5]
        .reshape(R, 2, 2, I, 2, micro, labels)
        .transpose(0, 2, 5, 3, 1, 4, 6)
        .reshape(n, own_labels)
        .astype(jnp.int32)
    )

    in_0.step()
    attend_out, feed_up, unused = lax.optimization_barrier((attend_out, feed_up, in_0.gathered))
    out_piece = grid.send(
        attend_out, lambda r, c, a, i, b: out_home(grid.flat(r, c, a, i, b))
    ).reshape(3 * share, width)
    ups = feed_up.reshape(2 * share, R, 2, 2, I, 2, hidden_share)
    ups = ups.transpose(2, 4, 0, 1, 3, 5, 6).reshape(G, 2 * share, hid)
    ups = grid.exchange(ups)
    blocks_2 = grid.exchange(in_blocks(attend_in[2].reshape(3 * share, width)))
    folds = hid // part

    def feed_bundle(which):
        up = ups[:, which * share : (which + 1) * share].reshape(-1, hid)
        return jnp.concatenate([up, fold(feed_down[which], hid)])

    def feed_weights(found, start=0, count=1, early=()):
        gathered, rows_at = found
        tall = G * share + hidden_share * width // hid
        if not kernels:
            gathered = jnp.take(gathered, rows_at, axis=0)[:, start:]
            gathered = unfold(gathered, tall)
            up = gathered[:, : G * share].reshape(R, 2, 2, 2, I, share, hid)
            down = unfold(gathered[:, G * share :], hidden_share)
            return up.transpose(0, 3, 1, 4, 2, 5, 6).reshape(width, hid), down.reshape(hid, width)
        moves = []
        for block in range(count):
            column, base = block * (hid // count), start + block * tall
            for k in range(K):
                for member in range(G):
                    first_row = base + member * share
                    moves.append((0, member_rows(k, member), column, k, first_row, share))
                for j in range(width // hid):
                    row = base + G * share + j * hidden_share
                    target = j * hid + column
                    moves.append((1, k * hidden_share, target, k, row, hidden_share))
        return place(gathered, rows_at, [(width, hid), (hid, width)], moves, early)

    def meta(query_docs, key_docs):
        return (key_docs[:, None], query_docs[:, None], places[:, None], places[None, :])

    source_meta = meta(source_row_docs, source_row_docs)
    target_meta = meta(target_row_docs, target_row_docs)
    cross_meta = meta(target_row_docs, source_row_docs)
    chip = 4 * tokens
    rows = I * chip

    order = Order()

    def launch(own):
        return own, grid.far_chips(own)

    def apply_near(launched, apply):
        chip_rows = order.use(grid.both_cores(launched[0]))
        return chip_rows, order.did(apply(chip_rows, 0))

    def apply_far(launched, apply):
        chips, results = [], []
        for k, array in enumerate(launched[1]):
            chips.append(order.use(grid.both_cores(order.use(array))))
            results.append(order.did(apply(chips[-1], k + 1)))
        return chips, results

    def apply_all(launched, apply):
        near, near_result = apply_near(launched, apply)
        chips, results = apply_far(launched, apply)
        return [near] + chips, [near_result] + results

    def send_far(parts, *early):
        joints = [grid.join_cores(array).astype(BF16) for array in parts]
        if early:
            joints[0] = gate(joints[0], *early)
        return [grid.return_chip(joint, k + 1) for k, joint in enumerate(joints)]

    def receive(near_part, sent):
        total = grid.join_cores(near_part)
        for array in sent:
            total = total + order.use(array).astype(F32)
        return total

    def attend_all(arrays, offsets, meta_rows, causal, early):
        mixed, exact, log_total = attend_call(
            arrays, offsets, meta_rows, causal, part, 0, rows, early
        )
        order.did(mixed)
        return [mixed[k * chip : (k + 1) * chip] for k in range(I)], (log_total, exact)

    def attend_far(arrays, offsets, meta_rows, causal, early=()):
        return attend_call(
            arrays, offsets, meta_rows, causal, part, chip, rows - chip, early
        )

    def attend_near(arrays, offsets, meta_rows, causal, early=()):
        return attend_call(arrays, offsets, meta_rows, causal, part, 0, chip, early)

    def by_far_chip(array):
        return [array[k * chip : (k + 1) * chip] for k in range(I - 1)]

    def stored(near, far):
        kept = (jnp.concatenate([near[2], far[2]], axis=2), jnp.concatenate([near[1], far[1]]))
        return [near[0]] + by_far_chip(far[0]), kept

    def far_product(array, weight):
        return [product(order.use(p), weight) for p in by_far_chip(array)]

    def projection(weight):
        return lambda array, unused: product(array, weight).astype(BF16)

    def rise(weight):
        def apply(normed, unused):
            up = product(normed, weight)
            return (up * gelu_gate(up)).astype(BF16)

        return apply

    self_offsets = (0, part, 2 * part)
    cross_offsets = (0, 0, part)

    out_all = Gathering(grid, out_piece, "arb")
    in_1 = Gathering(grid, first[:, 3 * share :].reshape(-1, part), "arb")
    in_order = jnp.arange(K, dtype=jnp.int32)
    enc_start = layer_norm(source, gains[0], biases[0])
    enc_normed = layer_norm(enc_start, gains[1], biases[1]).astype(BF16)
    in_0.step()
    out_all.step()
    in_1.step()
    feed_0 = Gathering(grid, feed_bundle(0), "abr")
    feed_0.step()
    enc_launched = launch(enc_normed)
    w_in_0 = natural_in(in_0.finish())
    enc_in, results = apply_all(enc_launched, projection(w_in_0))
    enc_qkv = jnp.concatenate(results)
    out_all.step()
    in_1.step()
    target = to_row(target_embed, w_in_0)
    dec_start = layer_norm(target, gains[4], biases[4])
    dec_normed = layer_norm(dec_start, gains[5], biases[5]).astype(BF16)
    dec_launched = launch(dec_normed)
    fed = feed_0.step()
    enc_source = ([enc_qkv] * 3, self_offsets, source_meta, False)
    far = attend_far(*enc_source, [fed])
    out_all.step()
    w_out = natural_out(out_all.finish())
    sent = send_far(far_product(far[0], w_out[0]))
    in_2 = Gathering(grid, blocks_2.reshape(-1, part), "abr")
    feed_1 = Gathering(grid, feed_bundle(1), "arb")
    near = attend_near(*enc_source, [in_2.step(), feed_1.step()])
    enc_mixed, enc_log = stored(near, far)
    in_1.step()
    w_in_1 = natural_in(in_1.finish())
    enc_near = product(near[0], w_out[0])
    dec_in, results = apply_all(dec_launched, projection(w_in_1))
    dec_qkv = jnp.concatenate(results)
    dec_source = ([dec_qkv] * 3, self_offsets, target_meta, True)
    enc_middle = enc_start + receive(enc_near, sent)
    ff_normed = layer_norm(enc_middle, gains[2], biases[2]).astype(BF16)
    enc_launched = launch(ff_normed)
    fed = feed_0.step()
    far = attend_far(*dec_source, [fed, in_2.step()])
    sent = send_far(far_product(far[0], w_out[1]))
    near = attend_near(*dec_source, [feed_1.step(), in_2.step()])
    dec_mixed, dec_log = stored(near, far)
    dec_self = dec_start + receive(product(near[0], w_out[1]), sent)
    cross_normed = layer_norm(dec_self, gains[6], biases[6]).astype(BF16)
    up_0, down_0 = feed_weights(feed_0.finish(), early=[feed_1.step()])
    ff_chips_0, hidden_0 = apply_all(enc_launched, rise(up_0))
    sent = send_far([product(h, down_0) for h in hidden_0[1:]])
    cross_launched = launch(cross_normed)
    enc_end = enc_middle + receive(product(order.use(hidden_0[0]), down_0), sent)
    encoded = order.did(layer_norm(enc_end, gains[3], biases[3]).astype(BF16))
    encoded_launched = launch(encoded)
    w_in_2 = natural_in(in_2.finish())
    cross_w_q, cross_w_kv = w_in_2[:, :part], w_in_2[:, part:]
    cross_in, results = apply_all(cross_launched, projection(cross_w_q))
    cross_q = jnp.concatenate(results)
    encoded_in, results = apply_all(encoded_launched, projection(cross_w_kv))
    cross_kv = jnp.concatenate(results)
    cross_source = ([cross_q, cross_kv, cross_kv], cross_offsets, cross_meta, False)
    far = attend_far(*cross_source)
    sent = send_far(far_product(far[0], w_out[2]))
    near = attend_near(*cross_source)
    cross_mixed, cross_log = stored(near, far)
    dec_cross = dec_self + receive(product(near[0], w_out[2]), sent)
    ff_normed = order.did(layer_norm(dec_cross, gains[7], biases[7]).astype(BF16))
    dec_launched = launch(ff_normed)
    up_1, down_1 = feed_weights(feed_1.finish())
    ff_chips_1, hidden_1 = apply_all(dec_launched, rise(up_1))
    sent = send_far([product(h, down_1) for h in hidden_1[1:]])
    dec_end = dec_cross + receive(product(order.use(hidden_1[0]), down_1), sent)
    final = order.did(layer_norm(dec_end, gains[8], biases[8]))

    all_rows = grid.everyone(jnp.take(final, label_rows, axis=0).astype(BF16))
    all_rows = all_rows.reshape(n * own_labels, width)
    every_token = every_token.reshape(-1)
    vocab_rows = vocab_table.shape[0]
    vocab_places = grid.me * vocab_rows + jnp.arange(vocab_rows, dtype=jnp.int32)
    logits = by_transpose(all_rows, vocab_table)
    target_hit = every_token[:, None] == vocab_places[None, :]
    row_max = jnp.max(logits, axis=-1)
    stats = jnp.stack(
        [
            row_max,
            jnp.sum(jnp.exp(logits - row_max[:, None]), axis=-1),
            jnp.sum(jnp.where(target_hit, logits, 0.0), axis=-1),
        ]
    )
    every_stats = grid.everyone(stats)
    joint = jnp.max(every_stats[:, 0], axis=0)
    total = jnp.sum(every_stats[:, 1] * jnp.exp(every_stats[:, 0] - joint), axis=0)
    stats = (joint, total, jnp.sum(every_stats[:, 2], axis=0))
    log_total = stats[0] + jnp.log(stats[1])
    mean_loss = jnp.sum(log_total - stats[2]) / (n * own_labels)
    grad_logits = (jnp.exp(logits - log_total[:, None]) - target_hit.astype(F32)).astype(BF16)
    grad_rows = product(grad_logits, vocab_table).reshape(n, own_labels, width)
    table_grad = rows_inner(grad_logits, all_rows)
    grad_rows = lax.all_to_all(grad_rows.astype(BF16), AXES, 0, 0)
    grad_rows = jnp.sum(grad_rows.astype(F32), axis=0)
    grad_final = jnp.zeros(final.shape, F32).at[label_rows].add(grad_rows)

    gain_grads = [None] * norms
    bias_grads = [None] * norms

    def back_norm(values, norm, gradient):
        result, gain_grads[norm], bias_grads[norm] = norm_back(values, gains[norm], gradient)
        return result

    def rows_sum(left, right):
        left, right = (
            order.use(a if not isinstance(a, list) else jnp.concatenate(a)) for a in (left, right)
        )
        return order.did(rows_inner(left, right).astype(BF16))

    def far_back(grads, weight, *early):
        return send_far([by_transpose(g, weight) for g in grads[1:]], *early)

    def near_back(grads, weight):
        return order.did(by_transpose(order.use(grads[0]), weight))

    def fall(chips, up_weight, down_weight):
        def apply(grad, k):
            up = product(chips[k], up_weight)
            return (by_transpose(grad, down_weight) * gelu_slope(up)).astype(BF16)

        return apply

    def back_projection(weight):
        return lambda grad, unused: by_transpose(grad, weight).astype(BF16)

    def attend_back(source, kept, grad_mixed, early=()):
        arrays, offsets, meta_rows, causal = source
        grad_mixed = jnp.concatenate(grad_mixed)
        return attend_back_call(
            arrays, offsets, meta_rows, causal, part, kept, grad_mixed, early
        )

    def by_chip(matrix):
        return [matrix[i * chip : (i + 1) * chip] for i in range(I)]

    def feed_bundle_grad(up_grad, down_grad):
        up_grad = up_grad.reshape(R, 2, 2, I, 2, share, hid)
        up_grad = up_grad.transpose(0, 2, 4, 1, 3, 5, 6).reshape(K, G * share, hid)
        down_grad = fold(down_grad.reshape(K, hidden_share, width), hid)
        return order.did(jnp.concatenate([up_grad, down_grad], axis=1))

    def row_sum(bundle):
        return lax.psum_scatter(bundle, ACROSS, scatter_dimension=0)

    def feed_steps(bundle, name):
        return Scattering(grid, bundle.reshape((R, 2, 2) + bundle.shape[1:]), name, (0, 1, 2))

    def settle_feed(total):
        up = grid.exchange(total[: G * share].reshape(G, share, hid).astype(BF16))
        up = up.reshape(2, I, share, R, 2, 2, hidden_share).transpose(2, 3, 0, 4, 1, 5, 6)
        return up.reshape(share, -1).astype(F32), unfold(total[G * share :].astype(F32), hidden_share)

    def in_scatter(grads, name):
        grads = grads.reshape(R, 2, 2, I, 2, share, 3 * part)
        return Scattering(grid, grads, name, (0, 2, 4))

    def in_rows(grads):
        grads = grads.reshape(R, 2, 2, I, 2, share, 3 * part).transpose(0, 2, 4, 1, 3, 5, 6)
        return grads.reshape(K, G * share, 3 * part)

    def settle_in(total):
        total = grid.exchange(total.reshape(G, share, 3 * part).astype(BF16)).astype(F32)
        return total.reshape(G, share, 3, part).transpose(2, 1, 0, 3).reshape(3, share, width)

    order.kept = True
    grad_dec_end = back_norm(dec_end, 8, grad_final)
    launched = launch(order.did(grad_dec_end.astype(BF16)))
    branch, grad_ups = apply_all(launched, fall(ff_chips_1, up_1, down_1))
    sent = far_back(grad_ups, up_1)
    near_part = near_back(grad_ups, up_1)
    feed_1 = feed_steps(feed_bundle_grad(rows_sum(ff_chips_1, grad_ups), rows_sum(hidden_1, branch)), "abr")
    feed_1.step(order.last)
    grad_dec_cross = grad_dec_end + back_norm(dec_cross, 7, receive(near_part, sent))

    launched = launch(order.did(grad_dec_cross.astype(BF16)))
    branch, grad_mixed = apply_all(launched, back_projection(w_out[2]))
    grads = attend_back(cross_source, cross_log, grad_mixed)
    grad_q, grad_kv = grads[:, :part], grads[:, part:]
    sent_kv = far_back(by_chip(grad_kv), cross_w_kv)
    sent_q = far_back(by_chip(grad_q), cross_w_q)
    near_kv = near_back(by_chip(grad_kv), cross_w_kv)
    near_q = near_back(by_chip(grad_q), cross_w_q)
    out_2 = rows_sum(cross_mixed, branch)
    grad_enc_end = back_norm(enc_end, 3, receive(near_kv, sent_kv))
    enc_launched = launch(order.did(grad_enc_end.astype(BF16)))
    in_grad_q = rows_sum(cross_in, grad_q)
    in_grad_kv = rows_sum(encoded_in, grad_kv)
    in_2 = in_scatter(jnp.concatenate([in_grad_q, in_grad_kv], axis=1), "arb")
    in_2.step(order.last)
    grad_dec_self = grad_dec_cross + back_norm(dec_self, 6, receive(near_q, sent_q))
    dec_launched = launch(order.did(grad_dec_self.astype(BF16)))
    feed_1.step(order.last)

    enc_branch, grad_ups = apply_all(enc_launched, fall(ff_chips_0, up_0, down_0))
    sent = far_back(grad_ups, up_0)
    near_part = near_back(grad_ups, up_0)
    feed_0 = feed_steps(feed_bundle_grad(rows_sum(ff_chips_0, grad_ups), rows_sum(hidden_0, enc_branch)), "abr")
    feed_0.step(order.last)
    in_2.step(order.last)
    grad_enc_middle = grad_enc_end + back_norm(enc_middle, 2, receive(near_part, sent))
    enc_launched = launch(order.did(grad_enc_middle.astype(BF16)))
    feed_1.step(order.last)
    dec_branch, grad_mixed = apply_all(dec_launched, back_projection(w_out[1]))
    grads_1 = attend_back(dec_source, dec_log, grad_mixed)
    in_2.step(order.last)

    branch, grad_mixed = apply_all(enc_launched, back_projection(w_out[0]))
    sent_1 = far_back(by_chip(grads_1), w_in_1)
    grads_0 = attend_back(enc_source, enc_log, grad_mixed)
    in_0 = in_scatter(rows_sum(enc_in, grads_0), "abr")
    given_0 = in_0.step()
    sent_0 = far_back(by_chip(grads_0), w_in_0, given_0)
    near_0 = near_back(by_chip(grads_0), w_in_0)
    near_1 = near_back(by_chip(grads_1), w_in_1)
    given = feed_0.step()
    in_1 = in_scatter(rows_sum(dec_in, grads_1), "arb")
    given_1 = in_1.step()
    grad_dec_start = grad_dec_self + back_norm(dec_start, 5, receive(near_1, sent_1))
    target_grad = from_row(back_norm(target, 4, grad_dec_start), given_1, given)
    grad_enc_start = grad_enc_middle + back_norm(enc_start, 1, receive(near_0, sent_0))
    source_grad = from_row(back_norm(source, 0, grad_enc_start), in_0.step())
    outs = [rows_sum(enc_mixed, branch), rows_sum(dec_mixed, dec_branch), out_2]
    out_grads = jnp.concatenate([g.reshape(R, 2, 2, share, width) for g in outs], axis=3)
    out_all = Scattering(grid, out_grads, "abr", (0, 1, 2))
    out_all.step(order.last)
    norm_grads = jnp.stack(gain_grads + bias_grads)
    norm_grads = norm_grads.reshape(2 * norms, n, share).transpose(1, 0, 2)
    norm_grads = lax.all_to_all(gate(norm_grads, in_0.step()), AXES, 0, 0)
    feed_0.step(order.last)
    in_1.step(order.last)

    def out_owner(r, c, a, i, b):
        block = (c * I + i) * K + (r * 2 + a) * 2 + b
        return (
            block // (8 * I),
            block // (4 * I) % 2,
            block // (2 * I) % 2,
            block // 2 % I,
            block % 2,
        )

    feed_1 = settle_feed(feed_1.finish()[0, 0, 0])
    in_2 = settle_in(in_2.finish())
    in_0 = settle_in(in_0.finish())
    in_1 = settle_in(in_1.finish())
    feed_0 = settle_feed(feed_0.finish()[0, 0, 0])
    attend_out_grad = grid.send(out_all.finish().reshape(3, share, width), out_owner)

    norm_grads = jnp.sum(norm_grads, axis=0)

    return (
        mean_loss,
        source_grad,
        target_grad,
        jnp.stack([in_0, in_1, in_2]),
        attend_out_grad,
        jnp.stack([feed_0[0], feed_1[0]]),
        jnp.stack([feed_0[1], feed_1[1]]),
        norm_grads[:norms],
        norm_grads[norms:],
        table_grad,
    )


def solution(mesh):
    dp, seq = mesh.shape["dp"], mesh.shape["seq"]
    mesh = jax.sharding.Mesh(mesh.devices.reshape(dp // 2, 2, 2, seq // 4, 2), AXES)

    def placed_local(*arrays):
        return local(dp, seq, *arrays)

    rows = P(None, ("r", "c"), ("a", "i", "b"), None)
    flat = P(None, ("r", "c"), ("a", "i", "b"))
    weight = P(None, AXES, None)
    weight_in = P(None, None, AXES, None)
    norm = P(None, AXES)
    table = P(AXES, None)
    return jax.shard_map(
        placed_local,
        mesh=mesh,
        in_specs=(
            (rows, rows, flat, flat, flat, flat)
            + (weight_in, weight, weight, weight, norm, norm, table)
        ),
        out_specs=(P(), rows, rows, weight_in, weight, weight, weight, norm, norm, table),
        check_vma=False,
    )
```
